512 devices in a mesh: row: 16 (over x, z_hi), col: 32 (over z_lo, y, core).
Axes of the slice: x: 4, y: 4, z: 16 (z_hi: 4, z_lo: 4; z = z_hi * 4 + z_lo), core: 2. Of those that a mesh axis runs over, the one named last changes fastest.
Arguments:
- iterate: bfloat16 [5120, 25600], P('row', 'col'), may hold values from -0.0175 to 0.0175
Outputs:
- update: float32 [5120, 25600], P('row', 'col')
The draws below stay inside these ranges and needn't reach their ends.
All inputs are finite; a program needn't handle non-finite values.
Results may differ from the reference program's by a relative error of at most 0.0035.
Values may be sent and summed in bfloat16 or wider, within the bound.
No kernel may reach another device: no remote copies, remote signals or barrier semaphores. Data moves between devices by JAX's collectives and lax.ppermute only.
A program may use at most 128 MiB of HBM per device.

```python
import math
import jax
import jax.numpy as jnp

M = 5120
N = 25600


def draw_iterate(key, part):
    key = jax.random.fold_in(key, 11)
    spread = 0.7 / math.sqrt(N)
    entries = jax.random.truncated_normal(key, -4.0, 4.0, (M, N), jnp.float32)
    return (entries * spread).astype(jnp.bfloat16)


def setup_inputs(seed: int = 0) -> dict:
    seeds = jax.random.split(jax.random.key(seed), 2)
    return {
        "iterate": draw_iterate(jax.random.fold_in(seeds[1], 71), 0),
    }


QUINTIC_A = 3.4445
QUINTIC_B = -4.775
QUINTIC_C = 2.0315

def reference(iterate):
    gram_matrix = jnp.dot(iterate, iterate.T, preferred_element_type=jnp.float32).astype(jnp.bfloat16)
    square = jnp.dot(gram_matrix, gram_matrix, preferred_element_type=jnp.float32)
    polynomial = (QUINTIC_B * gram_matrix.astype(jnp.float32) + QUINTIC_C * square).astype(jnp.bfloat16)
    product = jnp.dot(polynomial, iterate, preferred_element_type=jnp.float32)
    return 0.2 * math.sqrt(N) * (QUINTIC_A * iterate.astype(jnp.float32) + product)
```

```python
import math

import jax
import jax.numpy as jnp
from jax import lax
from jax.sharding import Mesh
from jax.sharding import PartitionSpec as P

QUINTIC_A = 3.4445
QUINTIC_B = -4.775
QUINTIC_C = 2.0315

SIZES = {"x": 4, "zh": 4, "zl": 4, "y": 4, "c": 2}
F32 = jnp.float32
BF16 = jnp.bfloat16


def take(value, axis, distance):
    n = lax.axis_size(axis)
    return lax.ppermute(value, axis, [((i + distance) % n, i) for i in range(n)])


def rolled(parts, start):
    stacked = jnp.stack(parts + parts[:-1])
    return lax.dynamic_slice_in_dim(stacked, start, len(parts), 0)


def ring(value, axis):
    cut = value.shape[0] // 2
    ahead = take(value, axis, 1)
    behind = take(value, axis, -1)
    first = take(ahead[:cut], axis, 1)
    second = take(behind[cut:], axis, -1)
    return [value, ahead, jnp.concatenate([first, second], 0), behind]


def gathered(value, axis):
    return rolled(ring(value, axis), (4 - lax.axis_index(axis)) % 4)


def exchanged_sum(value, axis):
    received = lax.all_to_all(value, axis, split_axis=0, concat_axis=0, tiled=True)
    return received.astype(F32).sum(0)


def local(iterate):
    rows, width = iterate.shape
    h, l = lax.axis_index("zh"), lax.axis_index("zl")
    x, c = lax.axis_index("x"), lax.axis_index("c")
    slab = rows // 4
    pair = 2 * rows

    mine = lax.all_gather(iterate, "x", axis=0, tiled=True)
    upper, lower = take(iterate, "zh", 1), take(iterate, "zh", -1)
    cut = rows // 2
    opposite = jnp.concatenate(
        [take(upper[:cut], "zh", 1), take(lower[cut:], "zh", -1)], 0
    )
    blocks = [iterate, upper, opposite, lower]
    keep = lax.dynamic_slice_in_dim(mine, c * pair, pair, 0)
    give = lax.dynamic_slice_in_dim(mine, (1 - c) * pair, pair, 0)

    def tile(block):
        sent = jnp.einsum("rn,sn->rs", block, give, preferred_element_type=F32).astype(BF16)
        other = take(sent, "c", 1)
        kept = jnp.einsum("rn,sn->rs", block, keep, preferred_element_type=F32)
        both = (kept + other.astype(F32)).astype(BF16)
        return exchanged_sum(both.reshape(4, slab, pair), "y").astype(BF16)

    tiles = {}
    for e in (0, 1, 3, 2):
        tiles[e] = tile(blocks[e])
    by_h = rolled([tiles[e] for e in range(4)], (4 - h) % 4)
    gram = exchanged_sum(by_h, "zl").astype(BF16)

    right_rows = jnp.concatenate(ring(gram, "zh"), axis=1)
    right = gathered(right_rows, "x").reshape(rows, 4 * pair)
    left_parts = []
    for t in range(4):
        route = [
            (((q + t) % 4) * 4 + p, p * 4 + q) for p in range(4) for q in range(4)
        ]
        left_parts.append(lax.ppermute(gram, ("zh", "zl"), route))
    left_rows = rolled(left_parts, (h - l) % 4)
    left = gathered(left_rows, "y")
    left = left.transpose(0, 2, 1, 3).reshape(rows, 4 * pair)
    square = jnp.einsum("jk,ik->ji", right, left, preferred_element_type=F32)
    own = jnp.where(x % 2 == 0, right[:, :rows], right[:, rows:pair]).astype(F32)
    own = jnp.where(x // 2 == c, own, 0.0)
    partial = QUINTIC_B * own + QUINTIC_C * square
    kept = lax.dynamic_slice_in_dim(partial, c * 2 * slab, 2 * slab, 0)
    sent = lax.dynamic_slice_in_dim(partial, (1 - c) * 2 * slab, 2 * slab, 0)
    polynomial = (kept + take(sent, "c", 1)).astype(BF16)

    spread = jnp.broadcast_to(polynomial[None], (4,) + polynomial.shape)
    by_l = lax.all_to_all(spread, "zl", split_axis=0, concat_axis=0, tiled=True)
    by_y = gathered(by_l, "y")
    by_c = lax.all_gather(by_y, "c", axis=0, tiled=False)
    polynomial_all = by_c.reshape(16 * rows, rows)

    by_e = rolled(blocks, (4 - h) % 4)
    column = lax.all_gather(by_e, "x", axis=0, tiled=False)
    column = column.reshape(2, 2, 4, 4, slab, width).transpose(0, 3, 2, 1, 4, 5)
    column = column.reshape(16 * rows, width)
    product = jnp.einsum("km,kn->mn", polynomial_all, column, preferred_element_type=F32)
    scale = 0.2 * math.sqrt(width * 32)
    return scale * (QUINTIC_A * iterate.astype(F32) + product)


def solution(mesh):
    fine = Mesh(mesh.devices.reshape(tuple(SIZES.values())), tuple(SIZES))
    spec = P(("x", "zh"), ("zl", "y", "c"))
    return jax.shard_map(local, mesh=fine, in_specs=(spec,), out_specs=spec, check_vma=False)
```

```python
import math

import jax
import jax.numpy as jnp
from jax import lax
from jax.sharding import Mesh
from jax.sharding import PartitionSpec as P

QUINTIC_A = 3.4445
QUINTIC_B = -4.775
QUINTIC_C = 2.0315

SIZES = {"x": 4, "zh": 4, "zl": 4, "y": 4, "c": 2}
Z = ("zh", "zl")
F32 = jnp.float32
BF16 = jnp.bfloat16


def take(value, axis, distance):
    n = lax.axis_size(axis)
    return lax.ppermute(value, axis, [((i + distance) % n, i) for i in range(n)])


def home(a, b):
    a, b = a % 4, b % 4
    if (a - b) % 4 == 2:
        return (b - 1) % 4 * 4 + (b + 1) % 4
    return b * 4 + a


def fetch(piece, wanted):
    route = [(home(*wanted(p, q)), p * 4 + q) for p in range(4) for q in range(4)]
    return lax.ppermute(piece, Z, route)


def rolled(parts, start):
    stacked = jnp.concatenate([parts, parts[:-1]], axis=0)
    return lax.dynamic_slice_in_dim(stacked, start, 4, 0)


def gathered(value, axis):
    spread = jnp.broadcast_to(value[None], (4,) + value.shape)
    return lax.all_to_all(spread, axis, split_axis=0, concat_axis=0, tiled=True)


def exchanged_sum(value, axis):
    received = lax.all_to_all(value, axis, split_axis=0, concat_axis=0, tiled=True)
    return received.astype(F32).sum(0)


def local(iterate):
    rows, width = iterate.shape
    h, x, c = lax.axis_index("zh"), lax.axis_index("x"), lax.axis_index("c")
    slab = rows // 4
    pair = 2 * rows

    def columns(block):
        halves = block.reshape(2, pair, width)
        return halves[c], halves[1 - c]

    def tile(block, keep, give):
        sent = jnp.einsum("rn,sn->rs", block, give, preferred_element_type=F32).astype(BF16)
        other = take(sent, "c", 1)
        kept = jnp.einsum("rn,sn->rs", block, keep, preferred_element_type=F32)
        both = (kept + other.astype(F32)).astype(BF16)
        return exchanged_sum(both.reshape(4, -1, pair), "y").astype(BF16)

    upper, lower = take(iterate, "zh", 1), take(iterate, "zh", -1)
    mine = gathered(iterate, "x")
    keep, give = columns(mine)
    level = tile(iterate, keep, give)

    upper, lower, level = lax.optimization_barrier((upper, lower, level))
    cut = rows // 2
    opposite = (take(upper[:cut], "zh", 1), take(lower[cut:], "zh", -1))
    above = gathered(upper, "x")
    both = jnp.stack([upper, lower]).reshape(2, 4, slab, width)
    both = both.transpose(1, 0, 2, 3).reshape(pair, width)
    sides = tile(both, keep, give).reshape(2, slab, pair)
    below = lax.all_gather(lower, "x", axis=0, tiled=False)
    across = tile(lower, *columns(above))

    tiles = jnp.stack([level, sides[0], across, sides[1]])
    gram = exchanged_sum(rolled(tiles, (4 - h) % 4), "zl").astype(BF16)

    opposite, gram = lax.optimization_barrier((opposite, gram))
    opposite = lax.all_gather(jnp.concatenate(opposite, 0), "x", axis=0, tiled=False)

    left = fetch(gram, lambda p, q: (p, q))
    right = {t: fetch(gram, lambda p, q, t=t: (q, p + t)) for t in (1, -1, 0)}
    left = rolled(gathered(left, "zl"), h)
    left = jnp.concatenate([left[e] for e in range(4)], axis=1)
    left = gathered(left, "y").reshape(rows, 4 * pair)
    cut = slab // 32 * 16
    far = jnp.concatenate([take(right[1][:cut], "zh", 1), take(right[-1][cut:], "zh", -1)], 0)
    right = jnp.concatenate([right[0], right[1], far, right[-1]], axis=1)
    right = gathered(right, "x").reshape(rows, 4 * pair)
    square = jnp.einsum("jk,ik->ji", right, left, preferred_element_type=F32)
    own = jnp.where(x % 2 == 0, right[:, :rows], right[:, rows:pair]).astype(F32)
    own = jnp.where(x // 2 == c, own, 0.0)
    partial = (QUINTIC_B * own + QUINTIC_C * square).reshape(2, 2 * slab, rows)
    polynomial = (partial[c] + take(partial[1 - c], "c", 1)).astype(BF16)

    polynomial = rolled(gathered(polynomial, "zl"), h)
    polynomial = gathered(polynomial, "y").reshape(8 * rows, rows)
    swapped = take(polynomial, "c", 1)

    column = jnp.stack([mine.reshape(4, rows, width), above.reshape(4, rows, width), opposite, below])
    column = column.reshape(4, 2, 2, 4, slab, width).transpose(1, 3, 0, 2, 4, 5)
    column = column.reshape(2, 8 * rows, width)
    product = jnp.einsum("km,kn->mn", polynomial, column[c], preferred_element_type=F32)
    product += jnp.einsum("km,kn->mn", swapped, column[1 - c], preferred_element_type=F32)
    scale = 0.2 * math.sqrt(width * 32)
    return scale * (QUINTIC_A * iterate.astype(F32) + product)


def solution(mesh):
    fine = Mesh(mesh.devices.reshape(tuple(SIZES.values())), tuple(SIZES))
    spec = P(("x", "zh"), ("zl", "y", "c"))
    return jax.shard_map(local, mesh=fine, in_specs=(spec,), out_specs=spec, check_vma=False)
```

```python
import math

import jax
import jax.numpy as jnp
from jax import lax
from jax.sharding import Mesh
from jax.sharding import PartitionSpec as P

QUINTIC_A = 3.4445
QUINTIC_B = -4.775
QUINTIC_C = 2.0315

SIZES = {"x": 4, "zh": 4, "zl": 4, "y": 4, "c": 2}
Z = ("zh", "zl")
F32 = jnp.float32
BF16 = jnp.bfloat16


def take(value, axis, distance):
    n = lax.axis_size(axis)
    return lax.ppermute(value, axis, [((i + distance) % n, i) for i in range(n)])


def home(a, b):
    if (a - b) % 4 == 2:
        return (b - 1) % 4 * 4 + (b + 1) % 4
    return b * 4 + a


def fetch(piece, wanted):
    route = [(home(*wanted(p, q)), p * 4 + q) for p in range(4) for q in range(4)]
    return lax.ppermute(piece, Z, route)


def rolled(parts, start):
    return [
        lax.select_n(start, *[parts[(s + i) % 4] for s in range(4)]) for i in range(4)
    ]


def gathered(value, axis):
    spread = jnp.broadcast_to(value[None], (lax.axis_size(axis),) + value.shape)
    return lax.all_to_all(spread, axis, split_axis=0, concat_axis=0, tiled=True)


def exchanged_sum(value, axis):
    received = lax.all_to_all(value, axis, split_axis=0, concat_axis=0, tiled=True)
    return received.astype(F32).sum(0)


def matmul_over_c(block, keep, give):
    sent = jnp.einsum("rn,sn->rs", block, give, preferred_element_type=F32).astype(BF16)
    other = take(sent, "c", 1)
    kept = jnp.einsum("rn,sn->rs", block, keep, preferred_element_type=F32)
    return (kept + other.astype(F32)).astype(BF16)


def local(iterate):
    rows, width = iterate.shape
    h, c = lax.axis_index("zh"), lax.axis_index("c")
    slab = rows // 4
    pair = 2 * rows

    def columns(block):
        halves = block.reshape(2, pair, -1)
        return halves[c], halves[1 - c]

    upper, lower = take(iterate, "zh", 1), take(iterate, "zh", -1)
    mine = lax.all_gather(iterate, "x", axis=0, tiled=True)
    above = lax.all_gather(upper, "x", axis=0, tiled=True)
    below = lax.all_gather(lower, "x", axis=0, tiled=True)
    cut = rows // 2
    odd = h % 2 == 1
    one = jnp.where(odd, upper, lower)[:cut]
    two = jnp.where(odd, lower, upper)[cut:]
    one = lax.all_gather(one, "zh", axis_index_groups=[[0, 1], [2, 3]])
    two = lax.all_gather(two, "zh", axis_index_groups=[[1, 2], [3, 0]])
    opposite = jnp.concatenate([one[1 - h % 2], two[h % 2]], axis=0)
    opposite = lax.all_gather(opposite, "x", axis=0, tiled=True)

    stacked = jnp.stack([iterate, upper, lower]).reshape(3, 4, slab, width)
    stacked = stacked.transpose(1, 0, 2, 3).reshape(3 * rows, width)
    tiles = matmul_over_c(stacked, *columns(mine))
    tiles = exchanged_sum(tiles.reshape(4, 3 * slab, pair), "y").astype(BF16)
    tiles = tiles.reshape(3, slab, pair)
    across = matmul_over_c(lower, *columns(above))
    across = exchanged_sum(across.reshape(4, slab, pair), "y").astype(BF16)
    by_l = jnp.stack(rolled([tiles[0], tiles[1], across, tiles[2]], (4 - h) % 4))
    gram = exchanged_sum(by_l, "zl").astype(BF16)

    turned = fetch(gram, lambda p, q: (p, q))
    gram = fetch(gram, lambda p, q: (q, p))
    left = gathered(gram, "zl").reshape(rows, pair)
    right = gathered(gram, ("x", "y")).reshape(2 * pair, pair)
    square = matmul_over_c(left, *columns(right))
    square = exchanged_sum(square.reshape(4, slab, pair), "zh")
    polynomial = (QUINTIC_B * turned.astype(F32) + QUINTIC_C * square).astype(BF16)

    polynomial = gathered(polynomial, "zl")
    polynomial = jnp.concatenate(rolled([polynomial[i] for i in range(4)], h), axis=1)
    polynomial = gathered(polynomial, "y").reshape(rows, 4 * pair)
    swapped = take(polynomial, "c", 1)

    blocks = [columns(block) for block in (mine, above, opposite, below)]
    own = jnp.concatenate([b[0] for b in blocks], axis=0)
    others = jnp.concatenate([b[1] for b in blocks], axis=0)
    product = jnp.einsum("mk,kn->mn", polynomial, own, preferred_element_type=F32)
    product += jnp.einsum("mk,kn->mn", swapped, others, preferred_element_type=F32)
    scale = 0.2 * math.sqrt(width * 32)
    return scale * (QUINTIC_A * iterate.astype(F32) + product)


def solution(mesh):
    fine = Mesh(mesh.devices.reshape(tuple(SIZES.values())), tuple(SIZES))
    spec = P(("x", "zh"), ("zl", "y", "c"))
    return jax.shard_map(local, mesh=fine, in_specs=(spec,), out_specs=spec, check_vma=False)
```

```python
import math

import jax
import jax.numpy as jnp
from jax import lax
from jax.sharding import Mesh
from jax.sharding import PartitionSpec as P

QUINTIC_A = 3.4445
QUINTIC_B = -4.775
QUINTIC_C = 2.0315

SIZES = {"x": 4, "zh": 4, "zl": 4, "y": 4, "c": 2}
Z = ("zh", "zl")
F32 = jnp.float32
BF16 = jnp.bfloat16


def take(value, axis, distance):
    n = lax.axis_size(axis)
    return lax.ppermute(value, axis, [((i + distance) % n, i) for i in range(n)])


def home(a, b):
    if (a - b) % 4 == 2:
        return (b - 1) % 4 * 4 + (b + 1) % 4
    return b * 4 + a


def fetch(piece, wanted):
    route = [(home(*wanted(p, q)), p * 4 + q) for p in range(4) for q in range(4)]
    return lax.ppermute(piece, Z, route)


def rolled(parts, start):
    return [
        lax.select_n(start, *[parts[(s + i) % 4] for s in range(4)]) for i in range(4)
    ]


def gathered(value, axis):
    spread = jnp.broadcast_to(value[None], (lax.axis_size(axis),) + value.shape)
    return lax.all_to_all(spread, axis, split_axis=0, concat_axis=0, tiled=True)


def around(value, axis):
    return [value] + [take(value, axis, distance) for distance in (1, 2, 3)]


def exchanged_sum(value, axis):
    received = lax.all_to_all(value, axis, split_axis=0, concat_axis=0, tiled=True)
    return received.astype(F32).sum(0)


def matmul_over_c(block, keep, give):
    sent = jnp.einsum("rn,sn->rs", block, give, preferred_element_type=F32).astype(BF16)
    other = take(sent, "c", 1)
    kept = jnp.einsum("rn,sn->rs", block, keep, preferred_element_type=F32)
    return (kept + other.astype(F32)).astype(BF16)


def local(iterate):
    rows, width = iterate.shape
    h, l, c = lax.axis_index("zh"), lax.axis_index("zl"), lax.axis_index("c")
    slab = rows // 4
    pair = 2 * rows

    def columns(block):
        halves = block.reshape(2, pair, -1)
        return halves[c], halves[1 - c]

    def tiles(block, others):
        part = jnp.einsum(
            "rn,csn->crs", block, others.reshape(2, pair, width), preferred_element_type=F32
        )
        part = part.astype(BF16).reshape(8, -1, pair)
        return exchanged_sum(part, ("c", "y")).astype(BF16).reshape(-1, slab, pair)

    upper, lower = take(iterate, "zh", 1), take(iterate, "zh", -1)
    upper, lower = lax.optimization_barrier((upper, lower))
    mine = lax.all_gather(iterate, "x", axis=0, tiled=True)
    above = lax.all_gather(upper, "x", axis=0, tiled=True)
    below = lax.all_gather(lower, "x", axis=0, tiled=True)
    cut = rows // 2
    opposite = [take(upper[:cut], "zh", 1), take(lower[cut:], "zh", -1)]
    opposite = lax.all_gather(jnp.concatenate(opposite, axis=0), "x", axis=0, tiled=True)

    stacked = jnp.stack([iterate, upper, lower]).reshape(3, 4, slab, width)
    near = tiles(stacked.transpose(1, 0, 2, 3).reshape(3 * rows, width), mine)
    across = tiles(lower, above)[0]
    by_l = jnp.stack(rolled([near[0], near[1], across, near[2]], (4 - h) % 4))
    gram = exchanged_sum(by_l, "zl").astype(BF16)

    turned = fetch(gram, lambda p, q: (p, q))
    gram = fetch(gram, lambda p, q: (q, p))
    left = jnp.concatenate(rolled(around(gram, "zl"), (4 - l) % 4), axis=0)
    right = gathered(gram, ("x", "y")).reshape(2 * pair, pair)
    square = matmul_over_c(left, *columns(right))
    square = exchanged_sum(square.reshape(4, slab, pair), "zh")
    polynomial = (QUINTIC_B * turned.astype(F32) + QUINTIC_C * square).astype(BF16)

    polynomial = jnp.concatenate(rolled(around(polynomial, "zl"), (h - l) % 4), axis=1)
    polynomial = gathered(polynomial, "y").reshape(rows, 4 * pair)
    swapped = take(polynomial, "c", 1)

    blocks = [columns(block) for block in (mine, above, opposite, below)]
    own = jnp.concatenate([b[0] for b in blocks], axis=0)
    others = jnp.concatenate([b[1] for b in blocks], axis=0)
    product = jnp.einsum("mk,kn->mn", polynomial, own, preferred_element_type=F32)
    product += jnp.einsum("mk,kn->mn", swapped, others, preferred_element_type=F32)
    scale = 0.2 * math.sqrt(width * 32)
    return scale * (QUINTIC_A * iterate.astype(F32) + product)


def solution(mesh):
    fine = Mesh(mesh.devices.reshape(tuple(SIZES.values())), tuple(SIZES))
    spec = P(("x", "zh"), ("zl", "y", "c"))
    return jax.shard_map(local, mesh=fine, in_specs=(spec,), out_specs=spec, check_vma=False)
```

```python
import functools
import math

import jax
import jax.numpy as jnp
from jax import lax
from jax.experimental import pallas as pl
from jax.experimental.pallas import tpu as pltpu
from jax.sharding import Mesh
from jax.sharding import PartitionSpec as P

QUINTIC_A = 3.4445
QUINTIC_B = -4.775
QUINTIC_C = 2.0315

SIZES = {"x": 4, "zh": 4, "zl": 4, "y": 4, "c": 2}
Z = ("zh", "zl")
F32 = jnp.float32
BF16 = jnp.bfloat16


def take(value, axis, distance):
    n = lax.axis_size(axis)
    return lax.ppermute(value, axis, [((i + distance) % n, i) for i in range(n)])


def home(a, b):
    if (a - b) % 4 == 2:
        return (b - 1) % 4 * 4 + (b + 1) % 4
    return b * 4 + a


def fetch(piece, wanted):
    route = [(home(*wanted(p, q)), p * 4 + q) for p in range(4) for q in range(4)]
    return lax.ppermute(piece, Z, route)


def rolled(parts, start):
    return [
        lax.select_n(start, *[parts[(s + i) % 4] for s in range(4)]) for i in range(4)
    ]


def gathered(value, axis):
    spread = jnp.broadcast_to(value[None], (lax.axis_size(axis),) + value.shape)
    return lax.all_to_all(spread, axis, split_axis=0, concat_axis=0, tiled=True)


def around(value, axis):
    return [value] + [take(value, axis, distance) for distance in (1, 2, 3)]


def exchanged_sum(value, axis):
    received = lax.all_to_all(value, axis, split_axis=0, concat_axis=0, tiled=True)
    return received.astype(F32).sum(0)


def matmul_over_c(block, keep, give):
    sent = jnp.einsum("rn,sn->rs", block, give, preferred_element_type=F32).astype(BF16)
    other = take(sent, "c", 1)
    kept = jnp.einsum("rn,sn->rs", block, keep, preferred_element_type=F32)
    return (kept + other.astype(F32)).astype(BF16)


def product_kernel(other, scale, *refs):
    total, left, *blocks, out, held, arrived = refs
    pair = left.shape[1] // 4
    c = lax.axis_index("c")
    start = pl.multiple_of((1 - c if other else c) * pair, pair)
    copies = [
        pltpu.make_async_copy(block.at[pl.ds(start, pair), :], held.at[e], arrived.at[e])
        for e, block in enumerate(blocks)
    ]
    for copy in copies:
        copy.start()
    value = total[...]
    for e, copy in enumerate(copies):
        copy.wait()
        value += jnp.dot(
            left[:, e * pair : (e + 1) * pair], held[e], preferred_element_type=F32
        )
    out[...] = scale * value


def add_product(other, scale, total, left, blocks):
    rows, width = total.shape
    pair = left.shape[1] // 4
    vmem = pl.BlockSpec(memory_space=pltpu.VMEM)
    return pl.pallas_call(
        functools.partial(product_kernel, other, scale),
        out_shape=jax.ShapeDtypeStruct(total.shape, F32),
        in_specs=[vmem, vmem] + [pl.BlockSpec(memory_space=pl.ANY)] * 4,
        out_specs=vmem,
        scratch_shapes=[
            pltpu.VMEM((4, pair, width), BF16),
            pltpu.SemaphoreType.DMA((4,)),
        ],
        cost_estimate=pl.CostEstimate(
            flops=2 * left.size * width,
            bytes_accessed=2 * left.size + 8 * pair * width + 8 * total.size,
            transcendentals=0,
        ),
        compiler_params=pltpu.CompilerParams(vmem_limit_bytes=32 * 2**20),
    )(total, left, *blocks)


def local(iterate):
    rows, width = iterate.shape
    h, l, c = lax.axis_index("zh"), lax.axis_index("zl"), lax.axis_index("c")
    slab = rows // 4
    pair = 2 * rows

    def columns(block):
        halves = block.reshape(2, pair, -1)
        return halves[c], halves[1 - c]

    def partial_tiles(block, others):
        part = jnp.einsum(
            "rn,csn->crs", block, others.reshape(2, pair, width), preferred_element_type=F32
        )
        return part.astype(BF16).reshape(8, -1, pair)

    def summed_tiles(part):
        return exchanged_sum(part, ("c", "y")).astype(BF16).reshape(-1, slab, pair)

    upper, lower = take(iterate, "zh", 1), take(iterate, "zh", -1)
    mine = lax.all_gather(iterate, "x", axis=0, tiled=True)
    upper, lower, mine = lax.optimization_barrier((upper, lower, mine))
    above = lax.all_gather(upper, "x", axis=0, tiled=True)
    below = lax.all_gather(lower, "x", axis=0, tiled=True)
    cut = rows // 2
    opposite = [take(upper[:cut], "zh", 1), take(lower[cut:], "zh", -1)]

    stacked = jnp.stack([iterate, upper, lower]).reshape(3, 4, slab, width)
    near = partial_tiles(stacked.transpose(1, 0, 2, 3).reshape(3 * rows, width), mine)
    near = summed_tiles(near)
    across = partial_tiles(lower, above)
    across, opposite = lax.optimization_barrier((across, opposite))
    across = summed_tiles(across)[0]
    opposite = lax.all_gather(jnp.concatenate(opposite, axis=0), "x", axis=0, tiled=True)

    by_l = jnp.stack(rolled([near[0], near[1], across, near[2]], (4 - h) % 4))
    gram = exchanged_sum(by_l, "zl").astype(BF16)

    turned = fetch(gram, lambda p, q: (p, q))
    gram = fetch(gram, lambda p, q: (q, p))
    left = jnp.concatenate(rolled(around(gram, "zl"), (4 - l) % 4), axis=0)
    right = gathered(gram, ("x", "y")).reshape(2 * pair, pair)
    square = matmul_over_c(left, *columns(right))
    square = exchanged_sum(square.reshape(4, slab, pair), "zh")
    polynomial = (QUINTIC_B * turned.astype(F32) + QUINTIC_C * square).astype(BF16)

    polynomial = gathered(polynomial, "zl")
    polynomial = jnp.concatenate(rolled([polynomial[i] for i in range(4)], h), axis=1)
    polynomial = gathered(polynomial, "y").reshape(rows, 4 * pair)
    swapped = take(polynomial, "c", 1)

    scale = 0.2 * math.sqrt(width * 32)
    blocks = (mine, above, opposite, below)
    total = QUINTIC_A * iterate.astype(F32)
    total = add_product(False, 1.0, total, polynomial, blocks)
    return add_product(True, scale, total, swapped, blocks)


def solution(mesh):
    fine = Mesh(mesh.devices.reshape(tuple(SIZES.values())), tuple(SIZES))
    spec = P(("x", "zh"), ("zl", "y", "c"))
    return jax.shard_map(local, mesh=fine, in_specs=(spec,), out_specs=spec, check_vma=False)
```

```python
import functools
import math

import jax
import jax.numpy as jnp
from jax import lax
from jax.experimental import pallas as pl
from jax.experimental.pallas import tpu as pltpu
from jax.sharding import Mesh
from jax.sharding import PartitionSpec as P

QUINTIC_A = 3.4445
QUINTIC_B = -4.775
QUINTIC_C = 2.0315

SIZES = {"x": 4, "zh": 4, "zl": 4, "y": 4, "c": 2}
Z = ("zh", "zl")
F32 = jnp.float32
BF16 = jnp.bfloat16


def take(value, axis, distance):
    n = lax.axis_size(axis)
    return lax.ppermute(value, axis, [((i + distance) % n, i) for i in range(n)])


def home(a, b):
    if (a - b) % 4 == 2:
        return (b - 1) % 4 * 4 + (b + 1) % 4
    return b * 4 + a


def fetch(piece, wanted):
    route = [(home(*wanted(p, q)), p * 4 + q) for p in range(4) for q in range(4)]
    return lax.ppermute(piece, Z, route)


def rolled(parts, start):
    return [
        lax.select_n(start, *[parts[(s + i) % 4] for s in range(4)]) for i in range(4)
    ]


def gathered(value, axis):
    spread = jnp.broadcast_to(value[None], (lax.axis_size(axis),) + value.shape)
    return lax.all_to_all(spread, axis, split_axis=0, concat_axis=0, tiled=True)


def around(value, axis):
    return [value] + [take(value, axis, distance) for distance in (1, 2, 3)]


def exchanged_sum(value, axis):
    received = lax.all_to_all(value, axis, split_axis=0, concat_axis=0, tiled=True)
    return received.astype(F32).sum(0)


def matmul_over_c(block, keep, give):
    sent = jnp.einsum("rn,sn->rs", block, give, preferred_element_type=F32).astype(BF16)
    other = take(sent, "c", 1)
    kept = jnp.einsum("rn,sn->rs", block, keep, preferred_element_type=F32)
    return (kept + other.astype(F32)).astype(BF16)


def product_kernel(other, total, left, *refs):
    *blocks, out = refs
    pair = left.shape[1] // 4
    c = lax.axis_index("c")
    start = pl.multiple_of((1 - c if other else c) * pair, pair)
    value = None
    for e, block in enumerate(blocks):
        part = jnp.dot(
            left[:, e * pair : (e + 1) * pair],
            block[pl.ds(start, pair), :],
            preferred_element_type=F32,
        )
        value = part if value is None else value + part
    if other:
        out[...] = 0.2 * math.sqrt(out.shape[1] * 32) * (total[...] + value)
    else:
        out[...] = QUINTIC_A * total[...].astype(F32) + value


def add_product(other, total, left, blocks):
    return pl.pallas_call(
        functools.partial(product_kernel, other),
        out_shape=jax.ShapeDtypeStruct(total.shape, F32),
        in_specs=[pl.BlockSpec(memory_space=pltpu.VMEM)] * 6,
        out_specs=pl.BlockSpec(memory_space=pltpu.VMEM),
        cost_estimate=pl.CostEstimate(
            flops=2 * left.size * total.shape[1],
            bytes_accessed=2 * left.size + 8 * total.size,
            transcendentals=0,
        ),
        compiler_params=pltpu.CompilerParams(vmem_limit_bytes=24 * 2**20),
    )(total, left, *blocks)


def local(iterate):
    rows, width = iterate.shape
    h, l, c = lax.axis_index("zh"), lax.axis_index("zl"), lax.axis_index("c")
    slab = rows // 4
    pair = 2 * rows

    def columns(block):
        halves = block.reshape(2, pair, -1)
        return halves[c], halves[1 - c]

    def partial_tiles(block, others):
        part = jnp.einsum(
            "rn,csn->crs", block, others.reshape(2, pair, width), preferred_element_type=F32
        )
        return part.astype(BF16).reshape(8, -1, pair)

    def summed_tiles(part):
        return exchanged_sum(part, ("c", "y")).astype(BF16).reshape(-1, slab, pair)

    upper, lower = take(iterate, "zh", 1), take(iterate, "zh", -1)
    mine = lax.all_gather(iterate, "x", axis=0, tiled=True)
    upper, lower, mine = lax.optimization_barrier((upper, lower, mine))
    above = lax.all_gather(upper, "x", axis=0, tiled=True)
    below = lax.all_gather(lower, "x", axis=0, tiled=True)
    cut = rows // 2
    opposite = [take(upper[:cut], "zh", 1), take(lower[cut:], "zh", -1)]

    stacked = jnp.stack([iterate, upper, lower]).reshape(3, 4, slab, width)
    near = partial_tiles(stacked.transpose(1, 0, 2, 3).reshape(3 * rows, width), mine)
    near = summed_tiles(near)
    across = partial_tiles(lower, above)
    across, opposite = lax.optimization_barrier((across, opposite))
    across = summed_tiles(across)[0]
    opposite = lax.all_gather(jnp.concatenate(opposite, axis=0), "x", axis=0, tiled=True)

    by_l = jnp.stack(rolled([near[0], near[1], across, near[2]], (4 - h) % 4))
    gram = exchanged_sum(by_l, "zl").astype(BF16)

    turned = fetch(gram, lambda p, q: (p, q))
    gram = fetch(gram, lambda p, q: (q, p))
    left = jnp.concatenate(rolled(around(gram, "zl"), (4 - l) % 4), axis=0)
    right = gathered(gram, ("x", "y")).reshape(2 * pair, pair)
    right, below = lax.optimization_barrier((right, below))
    square = matmul_over_c(left, *columns(right))
    square = exchanged_sum(square.reshape(4, slab, pair), "zh")
    square, opposite = lax.optimization_barrier((square, opposite))
    polynomial = (QUINTIC_B * turned.astype(F32) + QUINTIC_C * square).astype(BF16)

    polynomial = gathered(polynomial, "zl")
    polynomial = jnp.concatenate(rolled([polynomial[i] for i in range(4)], h), axis=1)
    polynomial = gathered(polynomial, "y").reshape(rows, 4 * pair)
    swapped = take(polynomial, "c", 1)

    blocks = (mine, above, opposite, below)
    total = add_product(False, iterate, polynomial, blocks)
    return add_product(True, total, swapped, blocks)


def solution(mesh):
    fine = Mesh(mesh.devices.reshape(tuple(SIZES.values())), tuple(SIZES))
    spec = P(("x", "zh"), ("zl", "y", "c"))
    return jax.shard_map(local, mesh=fine, in_specs=(spec,), out_specs=spec, check_vma=False)
```

```python
import functools
import math

import jax
import jax.numpy as jnp
from jax import lax
from jax.experimental import pallas as pl
from jax.experimental.pallas import tpu as pltpu
from jax.sharding import Mesh
from jax.sharding import PartitionSpec as P

QUINTIC_A = 3.4445
QUINTIC_B = -4.775
QUINTIC_C = 2.0315

SIZES = {"x": 4, "zh": 4, "zl": 4, "y": 4, "c": 2}
Z = ("zh", "zl")
F32 = jnp.float32
BF16 = jnp.bfloat16


def take(value, axis, distance):
    n = lax.axis_size(axis)
    return lax.ppermute(value, axis, [((i + distance) % n, i) for i in range(n)])


def home(a, b):
    if (a - b) % 4 == 2:
        return (b - 1) % 4 * 4 + (b + 1) % 4
    return b * 4 + a


def fetch(piece, wanted):
    route = [(home(*wanted(p, q)), p * 4 + q) for p in range(4) for q in range(4)]
    return lax.ppermute(piece, Z, route)


def rolled(parts, start):
    return [
        lax.select_n(start, *[parts[(s + i) % 4] for s in range(4)]) for i in range(4)
    ]


def gathered(value, axis):
    spread = jnp.broadcast_to(value[None], (lax.axis_size(axis),) + value.shape)
    return lax.all_to_all(spread, axis, split_axis=0, concat_axis=0, tiled=True)


def around(value, axis):
    return [value] + [take(value, axis, distance) for distance in (1, 2, 3)]


def exchanged_sum(value, axis):
    received = lax.all_to_all(value, axis, split_axis=0, concat_axis=0, tiled=True)
    return received.astype(F32).sum(0)


def matmul_over_c(block, keep, give):
    sent = jnp.einsum("rn,sn->rs", block, give, preferred_element_type=F32).astype(BF16)
    other = lax.all_gather(sent, "c", axis=0, tiled=False)[1 - lax.axis_index("c")]
    kept = jnp.einsum("rn,sn->rs", block, keep, preferred_element_type=F32)
    return (kept + other.astype(F32)).astype(BF16)


def product_kernel(other, total, left, *refs):
    *blocks, out = refs
    pair = left.shape[1] // 4
    c = lax.axis_index("c")
    start = pl.multiple_of((1 - c if other else c) * pair, pair)
    value = None
    for e, block in enumerate(blocks):
        part = jnp.dot(
            left[:, e * pair : (e + 1) * pair],
            block[pl.ds(start, pair), :],
            preferred_element_type=F32,
        )
        value = part if value is None else value + part
    if other:
        out[...] = 0.2 * math.sqrt(out.shape[1] * 32) * (total[...] + value)
    else:
        out[...] = QUINTIC_A * total[...].astype(F32) + value


def add_product(other, total, left, blocks):
    return pl.pallas_call(
        functools.partial(product_kernel, other),
        out_shape=jax.ShapeDtypeStruct(total.shape, F32),
        in_specs=[pl.BlockSpec(memory_space=pltpu.VMEM)] * 6,
        out_specs=pl.BlockSpec(memory_space=pltpu.VMEM),
        cost_estimate=pl.CostEstimate(
            flops=2 * left.size * total.shape[1],
            bytes_accessed=2 * left.size + 8 * total.size,
            transcendentals=0,
        ),
        compiler_params=pltpu.CompilerParams(vmem_limit_bytes=24 * 2**20),
    )(total, left, *blocks)


def local(iterate):
    rows, width = iterate.shape
    h, l, c = lax.axis_index("zh"), lax.axis_index("zl"), lax.axis_index("c")
    slab = rows // 4
    pair = 2 * rows

    def columns(block):
        halves = block.reshape(2, pair, -1)
        return halves[c], halves[1 - c]

    def partial_tiles(block, others):
        part = jnp.einsum(
            "rn,csn->crs", block, others.reshape(2, pair, width), preferred_element_type=F32
        )
        return part.astype(BF16).reshape(8, -1, pair)

    def summed_tiles(part):
        return exchanged_sum(part, ("c", "y")).astype(BF16).reshape(-1, slab, pair)

    upper, lower = take(iterate, "zh", 1), take(iterate, "zh", -1)
    mine = lax.all_gather(iterate, "x", axis=0, tiled=True)
    upper, lower, mine = lax.optimization_barrier((upper, lower, mine))
    above = lax.all_gather(upper, "x", axis=0, tiled=True)
    below = lax.all_gather(lower, "x", axis=0, tiled=True)
    cut = rows // 2
    opposite = [take(upper[:cut], "zh", 1), take(lower[cut:], "zh", -1)]

    stacked = jnp.stack([iterate, upper, lower]).reshape(3, 4, slab, width)
    near = partial_tiles(stacked.transpose(1, 0, 2, 3).reshape(3 * rows, width), mine)
    near = summed_tiles(near)
    across = partial_tiles(lower, above)
    across, opposite = lax.optimization_barrier((across, opposite))
    across = summed_tiles(across)[0]
    opposite = lax.all_gather(jnp.concatenate(opposite, axis=0), "x", axis=0, tiled=True)

    by_l = jnp.stack(rolled([near[0], near[1], across, near[2]], (4 - h) % 4))
    gram = exchanged_sum(by_l, "zl").astype(BF16)

    turned = fetch(gram, lambda p, q: (p, q))
    gram = fetch(gram, lambda p, q: (q, p))
    left = jnp.concatenate(rolled(around(gram, "zl"), (4 - l) % 4), axis=0)
    right = gathered(gram, ("x", "y")).reshape(2 * pair, pair)
    left, right, below, turned = lax.optimization_barrier((left, right, below, turned))
    square = matmul_over_c(left, *columns(right))
    square = exchanged_sum(square.reshape(4, slab, pair), "zh")
    square, opposite = lax.optimization_barrier((square, opposite))
    polynomial = (QUINTIC_B * turned.astype(F32) + QUINTIC_C * square).astype(BF16)

    polynomial = lax.all_gather(polynomial, "zl", axis=0, tiled=False)
    polynomial = jnp.concatenate(rolled([polynomial[i] for i in range(4)], h), axis=1)
    polynomial = gathered(polynomial, "y").reshape(rows, 4 * pair)
    swapped = take(polynomial, "c", 1)

    blocks = (mine, above, opposite, below)
    total = add_product(False, iterate, polynomial, blocks)
    return add_product(True, total, swapped, blocks)


def solution(mesh):
    fine = Mesh(mesh.devices.reshape(tuple(SIZES.values())), tuple(SIZES))
    spec = P(("x", "zh"), ("zl", "y", "c"))
    return jax.shard_map(local, mesh=fine, in_specs=(spec,), out_specs=spec, check_vma=False)
```

```python
import functools
import math

import jax
import jax.numpy as jnp
from jax import lax
from jax.experimental import pallas as pl
from jax.experimental.pallas import tpu as pltpu
from jax.sharding import Mesh
from jax.sharding import PartitionSpec as P

QUINTIC_A = 3.4445
QUINTIC_B = -4.775
QUINTIC_C = 2.0315

SIZES = {"x": 4, "zh": 4, "zl": 4, "y": 4, "c": 2}
F32 = jnp.float32
BF16 = jnp.bfloat16


def take(value, axis, distance):
    n = lax.axis_size(axis)
    return lax.ppermute(value, axis, [((i + distance) % n, i) for i in range(n)])


def rolled(parts, start):
    return [
        lax.select_n(start, *[parts[(s + i) % 4] for s in range(4)]) for i in range(4)
    ]


def gathered(value, axis):
    spread = jnp.broadcast_to(value[None], (lax.axis_size(axis),) + value.shape)
    return lax.all_to_all(spread, axis, split_axis=0, concat_axis=0, tiled=True)


def around(value, axis):
    return [value] + [take(value, axis, distance) for distance in (1, 2, 3)]


def exchanged_sum(value, axis):
    received = lax.all_to_all(value, axis, split_axis=0, concat_axis=0, tiled=True)
    return received.astype(F32).sum(0)


def matmul_over_c(block, keep, give):
    sent = jnp.einsum("rn,sn->rs", block, give, preferred_element_type=F32).astype(BF16)
    other = lax.all_gather(sent, "c", axis=0, tiled=False)[1 - lax.axis_index("c")]
    kept = jnp.einsum("rn,sn->rs", block, keep, preferred_element_type=F32)
    return (kept + other.astype(F32)).astype(BF16)


def product_kernel(other, total, left, *refs):
    *blocks, out = refs
    pair = left.shape[1] // 4
    c = lax.axis_index("c")
    start = pl.multiple_of((1 - c if other else c) * pair, pair)
    value = None
    for e, block in enumerate(blocks):
        part = jnp.dot(
            left[:, e * pair : (e + 1) * pair],
            block[pl.ds(start, pair), :],
            preferred_element_type=F32,
        )
        value = part if value is None else value + part
    if other:
        out[...] = 0.2 * math.sqrt(out.shape[1] * 32) * (total[...] + value)
    else:
        out[...] = QUINTIC_A * total[...].astype(F32) + value


def add_product(other, total, left, blocks):
    return pl.pallas_call(
        functools.partial(product_kernel, other),
        out_shape=jax.ShapeDtypeStruct(total.shape, F32),
        in_specs=[pl.BlockSpec(memory_space=pltpu.VMEM)] * 6,
        out_specs=pl.BlockSpec(memory_space=pltpu.VMEM),
        cost_estimate=pl.CostEstimate(
            flops=2 * left.size * total.shape[1],
            bytes_accessed=2 * left.size + 8 * total.size,
            transcendentals=0,
        ),
        compiler_params=pltpu.CompilerParams(vmem_limit_bytes=24 * 2**20),
    )(total, left, *blocks)


def local(iterate):
    rows, width = iterate.shape
    h, l, c = lax.axis_index("zh"), lax.axis_index("zl"), lax.axis_index("c")
    slab = rows // 4
    pair = 2 * rows

    def columns(block):
        halves = block.reshape(2, pair, -1)
        return halves[c], halves[1 - c]

    def partial_tiles(block, others):
        part = jnp.einsum(
            "rn,csn->crs", block, others.reshape(2, pair, width), preferred_element_type=F32
        )
        return part.astype(BF16).reshape(8, -1, pair)

    def summed_tiles(part):
        return exchanged_sum(part, ("c", "y")).astype(BF16).reshape(-1, slab, pair)

    upper, lower = take(iterate, "zh", 1), take(iterate, "zh", -1)
    mine = lax.all_gather(iterate, "x", axis=0, tiled=True)
    upper, lower, mine = lax.optimization_barrier((upper, lower, mine))
    above = lax.all_gather(upper, "x", axis=0, tiled=True)
    below = lax.all_gather(lower, "x", axis=0, tiled=True)
    cut = rows // 2
    opposite = lax.optimization_barrier((upper[:cut], lower[cut:]))
    opposite = (take(opposite[0], "zh", 1), take(opposite[1], "zh", -1))
    opposite = jnp.concatenate(lax.optimization_barrier(opposite), axis=0)

    sides = jnp.stack([iterate, upper, lower]).reshape(3, 4, slab, width)
    sides = partial_tiles(sides.transpose(1, 0, 2, 3).reshape(3 * rows, width), mine)
    sides = summed_tiles(sides)
    across = partial_tiles(opposite, mine)
    sides, across = lax.optimization_barrier((sides, across))
    across = summed_tiles(across)
    opposite = lax.all_gather(opposite, "x", axis=0, tiled=True)

    by_l = jnp.stack(rolled([sides[0], sides[1], across[0], sides[2]], (4 - h) % 4))
    gram = exchanged_sum(by_l, "zl").astype(BF16)

    turned = [(q * 4 + p, p * 4 + q) for p in range(4) for q in range(4)]
    turned = lax.ppermute(gram, ("zh", "zl"), turned)
    left = lax.all_gather(gram, "zl", axis=0, tiled=True)
    right = gathered(gram, ("x", "y")).reshape(2 * pair, pair)
    left, right, above, below, turned = lax.optimization_barrier(
        (left, right, above, below, turned)
    )
    square = matmul_over_c(left, *columns(right))
    square = exchanged_sum(square.reshape(4, slab, pair), "zh")
    square, opposite = lax.optimization_barrier((square, opposite))
    polynomial = (QUINTIC_B * turned.astype(F32) + QUINTIC_C * square).astype(BF16)

    polynomial = lax.all_gather(polynomial, "zl", axis=0, tiled=False)
    polynomial = jnp.concatenate(rolled([polynomial[i] for i in range(4)], h), axis=1)
    polynomial = gathered(polynomial, "y").reshape(rows, 4 * pair)
    swapped = take(polynomial, "c", 1)

    blocks = (mine, above, opposite, below)
    total = add_product(False, iterate, polynomial, blocks)
    return add_product(True, total, swapped, blocks)


def solution(mesh):
    fine = Mesh(mesh.devices.reshape(tuple(SIZES.values())), tuple(SIZES))
    spec = P(("x", "zh"), ("zl", "y", "c"))
    return jax.shard_map(local, mesh=fine, in_specs=(spec,), out_specs=spec, check_vma=False)
```

```python
import functools
import math

import jax
import jax.numpy as jnp
from jax import lax
from jax.experimental import pallas as pl
from jax.experimental.pallas import tpu as pltpu
from jax.sharding import Mesh
from jax.sharding import PartitionSpec as P

QUINTIC_A = 3.4445
QUINTIC_B = -4.775
QUINTIC_C = 2.0315

SIZES = {"x": 4, "zh": 4, "zl": 4, "y": 4, "c": 2}
F32 = jnp.float32
BF16 = jnp.bfloat16


def take(value, axis, distance):
    n = lax.axis_size(axis)
    return lax.ppermute(value, axis, [((i + distance) % n, i) for i in range(n)])


def rolled(parts, start):
    return [
        lax.select_n(start, *[parts[(s + i) % 4] for s in range(4)]) for i in range(4)
    ]


def gathered(value, axis):
    spread = jnp.broadcast_to(value[None], (lax.axis_size(axis),) + value.shape)
    return lax.all_to_all(spread, axis, split_axis=0, concat_axis=0, tiled=True)


def around(value, axis):
    return [value] + [take(value, axis, distance) for distance in (1, 2, 3)]


def exchanged(value, axis):
    return lax.all_to_all(value, axis, split_axis=0, concat_axis=0, tiled=True)


def exchanged_sum(value, axis):
    return exchanged(value, axis).astype(F32).sum(0)


def matmul_over_c(block, keep, give):
    sent = jnp.einsum("rn,sn->rs", block, give, preferred_element_type=F32).astype(BF16)
    other = lax.all_gather(sent, "c", axis=0, tiled=False)[1 - lax.axis_index("c")]
    kept = jnp.einsum("rn,sn->rs", block, keep, preferred_element_type=F32)
    return (kept + other.astype(F32)).astype(BF16)


def product_kernel(other, total, left, *refs):
    *blocks, out = refs
    pair = left.shape[1] // 4
    c = lax.axis_index("c")
    start = pl.multiple_of((1 - c if other else c) * pair, pair)
    value = None
    for e, block in enumerate(blocks):
        part = jnp.dot(
            left[:, e * pair : (e + 1) * pair],
            block[pl.ds(start, pair), :],
            preferred_element_type=F32,
        )
        value = part if value is None else value + part
    if other:
        out[...] = 0.2 * math.sqrt(out.shape[1] * 32) * (total[...] + value)
    else:
        out[...] = QUINTIC_A * total[...].astype(F32) + value


def add_product(other, total, left, blocks):
    return pl.pallas_call(
        functools.partial(product_kernel, other),
        out_shape=jax.ShapeDtypeStruct(total.shape, F32),
        in_specs=[pl.BlockSpec(memory_space=pltpu.VMEM)] * 6,
        out_specs=pl.BlockSpec(memory_space=pltpu.VMEM),
        cost_estimate=pl.CostEstimate(
            flops=2 * left.size * total.shape[1],
            bytes_accessed=2 * left.size + 8 * total.size,
            transcendentals=0,
        ),
        compiler_params=pltpu.CompilerParams(vmem_limit_bytes=24 * 2**20),
    )(total, left, *blocks)


def local(iterate):
    rows, width = iterate.shape
    h, l, c = lax.axis_index("zh"), lax.axis_index("zl"), lax.axis_index("c")
    slab = rows // 4
    pair = 2 * rows

    def columns(block):
        halves = block.reshape(2, pair, -1)
        return halves[c], halves[1 - c]

    def partial_tiles(block, others):
        part = jnp.einsum(
            "rn,csn->crs", block, others.reshape(2, pair, width), preferred_element_type=F32
        )
        return part.astype(BF16).reshape(8, -1, pair)

    def summed_tiles(parts):
        return parts.astype(F32).sum(0).astype(BF16).reshape(-1, slab, pair)

    upper, lower = take(iterate, "zh", 1), take(iterate, "zh", -1)
    mine = lax.all_gather(iterate, "x", axis=0, tiled=True)
    upper, lower, mine = lax.optimization_barrier((upper, lower, mine))
    above = lax.all_gather(upper, "x", axis=0, tiled=True)
    below = lax.all_gather(lower, "x", axis=0, tiled=True)
    cut = rows // 2
    opposite = lax.optimization_barrier((upper[:cut], lower[cut:]))
    opposite = (take(opposite[0], "zh", 1), take(opposite[1], "zh", -1))
    opposite = jnp.concatenate(lax.optimization_barrier(opposite), axis=0)

    sides = jnp.stack([iterate, upper, lower]).reshape(3, 4, slab, width)
    sides = partial_tiles(sides.transpose(1, 0, 2, 3).reshape(3 * rows, width), mine)
    sides = exchanged(sides, ("c", "y"))
    across = matmul_over_c(opposite, *columns(mine)).reshape(4, slab, pair)
    sides, across = lax.optimization_barrier((sides, across))
    sides, across = summed_tiles(sides), summed_tiles(exchanged(across, "y"))
    opposite = lax.all_gather(opposite, "x", axis=0, tiled=True)

    by_l = jnp.stack(rolled([sides[0], sides[1], across[0], sides[2]], (4 - h) % 4))
    gram = exchanged_sum(by_l, "zl").astype(BF16)

    turned = [(q * 4 + p, p * 4 + q) for p in range(4) for q in range(4)]
    turned = lax.ppermute(gram, ("zh", "zl"), turned)
    left = lax.all_gather(gram, "zl", axis=0, tiled=True)
    right = gathered(gram, ("x", "y")).reshape(2 * pair, pair)
    left, right, above, below, turned = lax.optimization_barrier(
        (left, right, above, below, turned)
    )
    square = matmul_over_c(left, *columns(right))
    square = exchanged_sum(square.reshape(4, slab, pair), "zh")
    square, opposite = lax.optimization_barrier((square, opposite))
    polynomial = (QUINTIC_B * turned.astype(F32) + QUINTIC_C * square).astype(BF16)

    polynomial = lax.all_gather(polynomial, "zl", axis=0, tiled=False)
    polynomial = jnp.concatenate(rolled([polynomial[i] for i in range(4)], h), axis=1)
    polynomial = gathered(polynomial, "y").reshape(rows, 4 * pair)
    swapped = take(polynomial, "c", 1)

    blocks = (mine, above, opposite, below)
    total = add_product(False, iterate, polynomial, blocks)
    return add_product(True, total, swapped, blocks)


def solution(mesh):
    fine = Mesh(mesh.devices.reshape(tuple(SIZES.values())), tuple(SIZES))
    spec = P(("x", "zh"), ("zl", "y", "c"))
    return jax.shard_map(local, mesh=fine, in_specs=(spec,), out_specs=spec, check_vma=False)
```

```python
import functools
import math

import jax
import jax.numpy as jnp
from jax import lax
from jax.experimental import pallas as pl
from jax.experimental.pallas import tpu as pltpu
from jax.sharding import Mesh
from jax.sharding import PartitionSpec as P

QUINTIC_A = 3.4445
QUINTIC_B = -4.775
QUINTIC_C = 2.0315

SIZES = {"x": 4, "zh": 4, "zl": 4, "y": 4, "c": 2}
F32 = jnp.float32
BF16 = jnp.bfloat16


def take(value, axis, distance):
    n = lax.axis_size(axis)
    return lax.ppermute(value, axis, [((i + distance) % n, i) for i in range(n)])


def shifted(value, step):
    route = [
        (h * 2 + c, (h + (step if c == 0 else -step)) % 4 * 2 + c)
        for h in range(4)
        for c in range(2)
    ]
    return lax.ppermute(value, ("zh", "c"), route)


def rolled(parts, start):
    return [
        lax.select_n(start, *[parts[(s + i) % 4] for s in range(4)]) for i in range(4)
    ]


def gathered(value, axis):
    spread = jnp.broadcast_to(value[None], (lax.axis_size(axis),) + value.shape)
    return lax.all_to_all(spread, axis, split_axis=0, concat_axis=0, tiled=True)


def around(value, axis):
    return [value] + [take(value, axis, distance) for distance in (1, 2, 3)]


def exchanged(value, axis):
    return lax.all_to_all(value, axis, split_axis=0, concat_axis=0, tiled=True)


def exchanged_sum(value, axis):
    return exchanged(value, axis).astype(F32).sum(0)


def matmul_over_c(block, keep, give):
    sent = jnp.einsum("rn,sn->rs", block, give, preferred_element_type=F32).astype(BF16)
    other = lax.all_gather(sent, "c", axis=0, tiled=False)[1 - lax.axis_index("c")]
    kept = jnp.einsum("rn,sn->rs", block, keep, preferred_element_type=F32)
    return (kept + other.astype(F32)).astype(BF16)


def product_kernel(other, total, left, *refs):
    *blocks, out = refs
    pair = left.shape[1] // 4
    c = lax.axis_index("c")
    start = pl.multiple_of((1 - c if other else c) * pair, pair)
    value = None
    for e, block in zip((0, 3 - 2 * c, 2, 1 + 2 * c), blocks):
        part = left[:, pl.ds(pl.multiple_of(e * pair, 128), pair)]
        part = jnp.dot(part, block[pl.ds(start, pair), :], preferred_element_type=F32)
        value = part if value is None else value + part
    if other:
        out[...] = 0.2 * math.sqrt(out.shape[1] * 32) * (total[...] + value)
    else:
        out[...] = QUINTIC_A * total[...].astype(F32) + value


def add_product(other, total, left, blocks):
    return pl.pallas_call(
        functools.partial(product_kernel, other),
        out_shape=jax.ShapeDtypeStruct(total.shape, F32),
        in_specs=[pl.BlockSpec(memory_space=pltpu.VMEM)] * 6,
        out_specs=pl.BlockSpec(memory_space=pltpu.VMEM),
        cost_estimate=pl.CostEstimate(
            flops=2 * left.size * total.shape[1],
            bytes_accessed=2 * left.size + 8 * total.size,
            transcendentals=0,
        ),
        compiler_params=pltpu.CompilerParams(vmem_limit_bytes=24 * 2**20),
    )(total, left, *blocks)


def local(iterate):
    rows, width = iterate.shape
    h, l, c = lax.axis_index("zh"), lax.axis_index("zl"), lax.axis_index("c")
    slab = rows // 4
    pair = 2 * rows

    def columns(block):
        halves = block.reshape(2, pair, -1)
        return halves[c], halves[1 - c]

    def partial_tiles(block, others):
        part = jnp.einsum(
            "rn,csn->crs", block, others.reshape(2, pair, width), preferred_element_type=F32
        )
        return part.astype(BF16).reshape(8, -1, pair)

    def summed_tiles(parts):
        return parts.astype(F32).sum(0).astype(BF16).reshape(-1, slab, pair)

    first, second = shifted(iterate, 1), shifted(iterate, -1)
    mine = lax.all_gather(iterate, "x", axis=0, tiled=True)
    first, second, mine = lax.optimization_barrier((first, second, mine))
    firsts = lax.all_gather(first, "x", axis=0, tiled=True)
    seconds = lax.all_gather(second, "x", axis=0, tiled=True)
    upper, lower = jnp.where(c == 0, second, first), jnp.where(c == 0, first, second)
    cut = rows // 2
    opposite = lax.optimization_barrier((first[:cut], second[cut:]))
    opposite = (shifted(opposite[0], 1), shifted(opposite[1], -1))
    opposite = jnp.concatenate(lax.optimization_barrier(opposite), axis=0)

    sides = jnp.stack([iterate, upper, lower]).reshape(3, 4, slab, width)
    sides = partial_tiles(sides.transpose(1, 0, 2, 3).reshape(3 * rows, width), mine)
    sides = exchanged(sides, ("c", "y"))
    across = matmul_over_c(opposite, *columns(mine)).reshape(4, slab, pair)
    sides, across = lax.optimization_barrier((sides, across))
    sides, across = summed_tiles(sides), summed_tiles(exchanged(across, "y"))
    opposite = lax.all_gather(opposite, "x", axis=0, tiled=True)

    by_l = jnp.stack(rolled([sides[0], sides[1], across[0], sides[2]], (4 - h) % 4))
    gram = exchanged_sum(by_l, "zl").astype(BF16)

    turned = [(q * 4 + p, p * 4 + q) for p in range(4) for q in range(4)]
    turned = lax.ppermute(gram, ("zh", "zl"), turned)
    left = lax.all_gather(gram, "zl", axis=0, tiled=True)
    right = gathered(gram, ("x", "y")).reshape(2 * pair, pair)
    left, right, firsts, seconds, turned = lax.optimization_barrier(
        (left, right, firsts, seconds, turned)
    )
    square = matmul_over_c(left, *columns(right))
    square = exchanged_sum(square.reshape(4, slab, pair), "zh")
    square, opposite = lax.optimization_barrier((square, opposite))
    polynomial = (QUINTIC_B * turned.astype(F32) + QUINTIC_C * square).astype(BF16)

    polynomial = lax.all_gather(polynomial, "zl", axis=0, tiled=False)
    polynomial = jnp.concatenate(rolled([polynomial[i] for i in range(4)], h), axis=1)
    polynomial = gathered(polynomial, "y").reshape(rows, 4 * pair)
    swapped = take(polynomial, "c", 1)

    blocks = (mine, firsts, opposite, seconds)
    total = add_product(False, iterate, polynomial, blocks)
    return add_product(True, total, swapped, blocks)


def solution(mesh):
    fine = Mesh(mesh.devices.reshape(tuple(SIZES.values())), tuple(SIZES))
    spec = P(("x", "zh"), ("zl", "y", "c"))
    return jax.shard_map(local, mesh=fine, in_specs=(spec,), out_specs=spec, check_vma=False)
```

```python
import functools
import math

import jax
import jax.numpy as jnp
from jax import lax
from jax.experimental import pallas as pl
from jax.experimental.pallas import tpu as pltpu
from jax.sharding import Mesh
from jax.sharding import PartitionSpec as P

QUINTIC_A = 3.4445
QUINTIC_B = -4.775
QUINTIC_C = 2.0315

SIZES = {"x": 4, "zh": 4, "zl": 4, "y": 4, "c": 2}
F32 = jnp.float32
BF16 = jnp.bfloat16


def take(value, axis, distance):
    n = lax.axis_size(axis)
    return lax.ppermute(value, axis, [((i + distance) % n, i) for i in range(n)])


def shifted(value, step):
    route = [
        (h * 2 + c, (h + (step if c == 0 else -step)) % 4 * 2 + c)
        for h in range(4)
        for c in range(2)
    ]
    return lax.ppermute(value, ("zh", "c"), route)


def rolled(parts, start):
    return [
        lax.select_n(start, *[parts[(s + i) % 4] for s in range(4)]) for i in range(4)
    ]


def gathered(value, axis):
    spread = jnp.broadcast_to(value[None], (lax.axis_size(axis),) + value.shape)
    return lax.all_to_all(spread, axis, split_axis=0, concat_axis=0, tiled=True)


def around(value, axis):
    return [value] + [take(value, axis, distance) for distance in (1, 2, 3)]


def exchanged(value, axis):
    return lax.all_to_all(value, axis, split_axis=0, concat_axis=0, tiled=True)


def exchanged_sum(value, axis):
    return exchanged(value, axis).astype(F32).sum(0)


def matmul_over_c(block, keep, give):
    sent = jnp.einsum("rn,sn->rs", block, give, preferred_element_type=F32).astype(BF16)
    other = lax.all_gather(sent, "c", axis=0, tiled=False)[1 - lax.axis_index("c")]
    kept = jnp.einsum("rn,sn->rs", block, keep, preferred_element_type=F32)
    return (kept + other.astype(F32)).astype(BF16)


def product_kernel(other, total, left, *refs):
    *blocks, out = refs
    pair = left.shape[1] // 4
    c = lax.axis_index("c")
    start = pl.multiple_of((1 - c if other else c) * pair, pair)
    value = None
    for e, block in enumerate(blocks):
        part = jnp.dot(
            left[:, e * pair : (e + 1) * pair],
            block[pl.ds(start, pair), :],
            preferred_element_type=F32,
        )
        value = part if value is None else value + part
    if other:
        out[...] = 0.2 * math.sqrt(out.shape[1] * 32) * (total[...] + value)
    else:
        out[...] = QUINTIC_A * total[...].astype(F32) + value


def add_product(other, total, left, blocks):
    return pl.pallas_call(
        functools.partial(product_kernel, other),
        out_shape=jax.ShapeDtypeStruct(total.shape, F32),
        in_specs=[pl.BlockSpec(memory_space=pltpu.VMEM)] * 6,
        out_specs=pl.BlockSpec(memory_space=pltpu.VMEM),
        cost_estimate=pl.CostEstimate(
            flops=2 * left.size * total.shape[1],
            bytes_accessed=2 * left.size + 8 * total.size,
            transcendentals=0,
        ),
        compiler_params=pltpu.CompilerParams(vmem_limit_bytes=24 * 2**20),
    )(total, left, *blocks)


def local(iterate):
    rows, width = iterate.shape
    h, l, c = lax.axis_index("zh"), lax.axis_index("zl"), lax.axis_index("c")
    slab = rows // 4
    pair = 2 * rows

    def columns(block):
        halves = block.reshape(2, pair, -1)
        return halves[c], halves[1 - c]

    def partial_tiles(block, others):
        part = jnp.einsum(
            "rn,csn->crs", block, others.reshape(2, pair, width), preferred_element_type=F32
        )
        return part.astype(BF16).reshape(8, -1, pair)

    def summed_tiles(parts):
        return parts.astype(F32).sum(0).astype(BF16).reshape(-1, slab, pair)

    upper, lower = take(iterate, "zh", 1), take(iterate, "zh", -1)
    mine = lax.all_gather(iterate, "x", axis=0, tiled=True)
    upper, lower, mine = lax.optimization_barrier((upper, lower, mine))
    above = lax.all_gather(upper, "x", axis=0, tiled=True)
    below = lax.all_gather(lower, "x", axis=0, tiled=True)
    cut = rows // 2
    opposite = lax.optimization_barrier((
        jnp.where(c == 0, lower[:cut], upper[:cut]),
        jnp.where(c == 0, upper[cut:], lower[cut:]),
    ))
    opposite = (shifted(opposite[0], 1), shifted(opposite[1], -1))
    opposite = jnp.concatenate(lax.optimization_barrier(opposite), axis=0)

    sides = jnp.stack([iterate, upper, lower]).reshape(3, 4, slab, width)
    sides = partial_tiles(sides.transpose(1, 0, 2, 3).reshape(3 * rows, width), mine)
    sides = exchanged(sides, ("c", "y"))
    across = matmul_over_c(opposite, *columns(mine)).reshape(4, slab, pair)
    sides, across = lax.optimization_barrier((sides, across))
    sides, across = summed_tiles(sides), summed_tiles(exchanged(across, "y"))
    opposite = lax.all_gather(opposite, "x", axis=0, tiled=True)

    by_l = jnp.stack(rolled([sides[0], sides[1], across[0], sides[2]], (4 - h) % 4))
    gram = exchanged_sum(by_l, "zl").astype(BF16)

    turned = [(q * 4 + p, p * 4 + q) for p in range(4) for q in range(4)]
    turned = lax.ppermute(gram, ("zh", "zl"), turned)
    left = lax.all_gather(gram, "zl", axis=0, tiled=True)
    right = gathered(gram, ("x", "y")).reshape(2 * pair, pair)
    left, right, above, below, turned = lax.optimization_barrier(
        (left, right, above, below, turned)
    )
    square = matmul_over_c(left, *columns(right))
    square = exchanged_sum(square.reshape(4, slab, pair), "zh")
    square, opposite = lax.optimization_barrier((square, opposite))
    polynomial = (QUINTIC_B * turned.astype(F32) + QUINTIC_C * square).astype(BF16)

    polynomial = lax.all_gather(polynomial, "zl", axis=0, tiled=False)
    polynomial = jnp.concatenate(rolled([polynomial[i] for i in range(4)], h), axis=1)
    polynomial = gathered(polynomial, "y").reshape(rows, 4 * pair)
    swapped = take(polynomial, "c", 1)

    blocks = (mine, above, opposite, below)
    total = add_product(False, iterate, polynomial, blocks)
    return add_product(True, total, swapped, blocks)


def solution(mesh):
    fine = Mesh(mesh.devices.reshape(tuple(SIZES.values())), tuple(SIZES))
    spec = P(("x", "zh"), ("zl", "y", "c"))
    return jax.shard_map(local, mesh=fine, in_specs=(spec,), out_specs=spec, check_vma=False)
```

```python
import functools
import math

import jax
import jax.numpy as jnp
from jax import lax
from jax.experimental import pallas as pl
from jax.experimental.pallas import tpu as pltpu
from jax.sharding import Mesh
from jax.sharding import PartitionSpec as P

QUINTIC_A = 3.4445
QUINTIC_B = -4.775
QUINTIC_C = 2.0315

SIZES = {"x": 4, "zh": 4, "zl": 4, "y": 4, "c": 2}
F32 = jnp.float32
BF16 = jnp.bfloat16


def take(value, axis, distance):
    n = lax.axis_size(axis)
    return lax.ppermute(value, axis, [((i + distance) % n, i) for i in range(n)])


def shifted(value, step):
    route = [
        (h * 2 + c, (h + (step if c == 0 else -step)) % 4 * 2 + c)
        for h in range(4)
        for c in range(2)
    ]
    return lax.ppermute(value, ("zh", "c"), route)


def rolled(parts, start):
    return [
        lax.select_n(start, *[parts[(s + i) % 4] for s in range(4)]) for i in range(4)
    ]


def gathered(value, axis):
    spread = jnp.broadcast_to(value[None], (lax.axis_size(axis),) + value.shape)
    return lax.all_to_all(spread, axis, split_axis=0, concat_axis=0, tiled=True)


def around(value, axis):
    return [value] + [take(value, axis, distance) for distance in (1, 2, 3)]


def exchanged(value, axis):
    return lax.all_to_all(value, axis, split_axis=0, concat_axis=0, tiled=True)


def exchanged_sum(value, axis):
    return exchanged(value, axis).astype(F32).sum(0)


def matmul_over_c(block, keep, give):
    sent = jnp.einsum("rn,sn->rs", block, give, preferred_element_type=F32).astype(BF16)
    other = lax.all_gather(sent, "c", axis=0, tiled=False)[1 - lax.axis_index("c")]
    kept = jnp.einsum("rn,sn->rs", block, keep, preferred_element_type=F32)
    return (kept + other.astype(F32)).astype(BF16)


def product_kernel(other, total, left, *refs):
    *blocks, out = refs
    pair = left.shape[1] // 4
    c = lax.axis_index("c")
    start = pl.multiple_of((1 - c if other else c) * pair, pair)
    value = None
    for e, block in enumerate(blocks):
        part = jnp.dot(
            left[:, e * pair : (e + 1) * pair],
            block[pl.ds(start, pair), :],
            preferred_element_type=F32,
        )
        value = part if value is None else value + part
    if other:
        out[...] = 0.2 * math.sqrt(out.shape[1] * 32) * (total[...] + value)
    else:
        out[...] = QUINTIC_A * total[...].astype(F32) + value


def add_product(other, total, left, blocks):
    return pl.pallas_call(
        functools.partial(product_kernel, other),
        out_shape=jax.ShapeDtypeStruct(total.shape, F32),
        in_specs=[pl.BlockSpec(memory_space=pltpu.VMEM)] * 6,
        out_specs=pl.BlockSpec(memory_space=pltpu.VMEM),
        cost_estimate=pl.CostEstimate(
            flops=2 * left.size * total.shape[1],
            bytes_accessed=2 * left.size + 8 * total.size,
            transcendentals=0,
        ),
        compiler_params=pltpu.CompilerParams(vmem_limit_bytes=24 * 2**20),
    )(total, left, *blocks)


def local(iterate):
    rows, width = iterate.shape
    h, l, c = lax.axis_index("zh"), lax.axis_index("zl"), lax.axis_index("c")
    slab = rows // 4
    pair = 2 * rows

    def columns(block):
        halves = block.reshape(2, pair, -1)
        return halves[c], halves[1 - c]

    def partial_tiles(block, others):
        part = jnp.einsum(
            "rn,csn->crs", block, others.reshape(2, pair, width), preferred_element_type=F32
        )
        return part.astype(BF16).reshape(8, -1, pair)

    def summed_tiles(parts):
        return parts.astype(F32).sum(0).astype(BF16).reshape(-1, slab, pair)

    upper, lower = take(iterate, "zh", 1), take(iterate, "zh", -1)
    mine = lax.all_gather(iterate, "x", axis=0, tiled=True)
    upper, lower, mine = lax.optimization_barrier((upper, lower, mine))
    above = lax.all_gather(upper, "x", axis=0, tiled=True)
    below = lax.all_gather(lower, "x", axis=0, tiled=True)
    cut = rows // 2
    opposite = lax.optimization_barrier((
        jnp.where(c == 0, lower[:cut], upper[:cut]),
        jnp.where(c == 0, upper[cut:], lower[cut:]),
    ))
    opposite = (shifted(opposite[0], 1), shifted(opposite[1], -1))
    opposite = jnp.concatenate(lax.optimization_barrier(opposite), axis=0)

    sides = jnp.stack([iterate, upper, lower]).reshape(3, 4, slab, width)
    sides = partial_tiles(sides.transpose(1, 0, 2, 3).reshape(3 * rows, width), mine)
    sides = exchanged(sides, ("c", "y"))
    across = matmul_over_c(opposite, *columns(mine)).reshape(4, slab, pair)
    sides, across = lax.optimization_barrier((sides, across))
    sides, across = summed_tiles(sides), summed_tiles(exchanged(across, "y"))
    opposite = lax.all_gather(opposite, "x", axis=0, tiled=True)

    by_l = jnp.stack(rolled([sides[0], sides[1], across[0], sides[2]], (4 - h) % 4))
    gram = exchanged_sum(by_l, "zl").astype(BF16)

    turned = [(q * 4 + p, p * 4 + q) for p in range(4) for q in range(4)]
    turned = lax.ppermute(gram, ("zh", "zl"), turned)
    left = lax.all_gather(gram, "zl", axis=0, tiled=True)
    right = gathered(gram, ("x", "y")).reshape(2 * pair, pair)
    left, right, above, below, turned = lax.optimization_barrier(
        (left, right, above, below, turned)
    )
    square = jnp.einsum("rn,csn->crs", left, right.reshape(2, pair, pair), preferred_element_type=F32)
    other = lax.all_gather(square[1 - c].astype(BF16), "c", axis=0, tiled=False)[1 - c]
    square = (square[c] + other.astype(F32)).astype(BF16)
    square = exchanged_sum(square.reshape(4, slab, pair), "zh")
    square, opposite = lax.optimization_barrier((square, opposite))
    polynomial = (QUINTIC_B * turned.astype(F32) + QUINTIC_C * square).astype(BF16)

    polynomial = lax.all_gather(polynomial, "zl", axis=0, tiled=False)
    polynomial = jnp.concatenate(rolled([polynomial[i] for i in range(4)], h), axis=1)
    polynomial = gathered(polynomial, "y").reshape(rows, 4 * pair)
    swapped = take(polynomial, "c", 1)

    blocks = (mine, above, opposite, below)
    total = add_product(False, iterate, polynomial, blocks)
    return add_product(True, total, swapped, blocks)


def solution(mesh):
    fine = Mesh(mesh.devices.reshape(tuple(SIZES.values())), tuple(SIZES))
    spec = P(("x", "zh"), ("zl", "y", "c"))
    return jax.shard_map(local, mesh=fine, in_specs=(spec,), out_specs=spec, check_vma=False)
```

```python
import functools
import math

import jax
import jax.numpy as jnp
from jax import lax
from jax.experimental import pallas as pl
from jax.experimental.pallas import tpu as pltpu
from jax.sharding import Mesh
from jax.sharding import PartitionSpec as P

QUINTIC_A = 3.4445
QUINTIC_B = -4.775
QUINTIC_C = 2.0315

SIZES = {"x": 4, "zh": 4, "zl": 4, "y": 4, "c": 2}
F32 = jnp.float32
BF16 = jnp.bfloat16


def take(value, axis, distance):
    n = lax.axis_size(axis)
    return lax.ppermute(value, axis, [((i + distance) % n, i) for i in range(n)])


def shifted(value, step):
    route = [
        (h * 2 + c, (h + (step if c == 0 else -step)) % 4 * 2 + c)
        for h in range(4)
        for c in range(2)
    ]
    return lax.ppermute(value, ("zh", "c"), route)


def rolled(parts, start):
    return [
        lax.select_n(start, *[parts[(s + i) % 4] for s in range(4)]) for i in range(4)
    ]


def gathered(value, axis):
    spread = jnp.broadcast_to(value[None], (lax.axis_size(axis),) + value.shape)
    return lax.all_to_all(spread, axis, split_axis=0, concat_axis=0, tiled=True)


def around(value, axis):
    return [value] + [take(value, axis, distance) for distance in (1, 2, 3)]


def exchanged(value, axis):
    return lax.all_to_all(value, axis, split_axis=0, concat_axis=0, tiled=True)


def exchanged_sum(value, axis):
    return exchanged(value, axis).astype(F32).sum(0)


def matmul_over_c(block, keep, give):
    sent = jnp.einsum("rn,sn->rs", block, give, preferred_element_type=F32).astype(BF16)
    other = lax.all_gather(sent, "c", axis=0, tiled=False)[1 - lax.axis_index("c")]
    kept = jnp.einsum("rn,sn->rs", block, keep, preferred_element_type=F32)
    return (kept + other.astype(F32)).astype(BF16)


def product_kernel(other, total, left, *refs):
    *blocks, out = refs
    pair = left.shape[1] // 4
    c = lax.axis_index("c")
    start = pl.multiple_of((1 - c if other else c) * pair, pair)
    value = None
    for e, block in enumerate(blocks):
        part = jnp.dot(
            left[:, e * pair : (e + 1) * pair],
            block[pl.ds(start, pair), :],
            preferred_element_type=F32,
        )
        value = part if value is None else value + part
    if other:
        out[...] = 0.2 * math.sqrt(out.shape[1] * 32) * (total[...] + value)
    else:
        out[...] = QUINTIC_A * total[...].astype(F32) + value


def add_product(other, total, left, blocks):
    return pl.pallas_call(
        functools.partial(product_kernel, other),
        out_shape=jax.ShapeDtypeStruct(total.shape, F32),
        in_specs=[pl.BlockSpec(memory_space=pltpu.VMEM)] * 6,
        out_specs=pl.BlockSpec(memory_space=pltpu.VMEM),
        cost_estimate=pl.CostEstimate(
            flops=2 * left.size * total.shape[1],
            bytes_accessed=2 * left.size + 8 * total.size,
            transcendentals=0,
        ),
        compiler_params=pltpu.CompilerParams(vmem_limit_bytes=24 * 2**20),
    )(total, left, *blocks)


def local(iterate):
    rows, width = iterate.shape
    h, l, c = lax.axis_index("zh"), lax.axis_index("zl"), lax.axis_index("c")
    slab = rows // 4
    pair = 2 * rows

    def columns(block):
        halves = block.reshape(2, pair, -1)
        return halves[c], halves[1 - c]

    def partial_tiles(block, others):
        part = jnp.einsum(
            "rn,csn->crs", block, others.reshape(2, pair, width), preferred_element_type=F32
        )
        return part.astype(BF16).reshape(8, -1, pair)

    def summed_tiles(parts):
        return parts.astype(F32).sum(0).astype(BF16).reshape(-1, slab, pair)

    upper, lower = take(iterate, "zh", 1), take(iterate, "zh", -1)
    mine = lax.all_gather(iterate, "x", axis=0, tiled=True)
    upper, lower, mine = lax.optimization_barrier((upper, lower, mine))
    above = lax.all_gather(upper, "x", axis=0, tiled=True)
    below = lax.all_gather(lower, "x", axis=0, tiled=True)
    cut = rows // 2
    opposite = lax.optimization_barrier((
        jnp.where(c == 0, lower[:cut], upper[:cut]),
        jnp.where(c == 0, upper[cut:], lower[cut:]),
    ))
    opposite = (shifted(opposite[0], 1), shifted(opposite[1], -1))
    opposite = jnp.concatenate(lax.optimization_barrier(opposite), axis=0)

    sides = jnp.stack([iterate, upper, lower]).reshape(3, 4, slab, width)
    sides = partial_tiles(sides.transpose(1, 0, 2, 3).reshape(3 * rows, width), mine)
    sides = exchanged(sides, ("c", "y"))
    across = matmul_over_c(opposite, *columns(mine)).reshape(4, slab, pair)
    sides, across = lax.optimization_barrier((sides, across))
    sides, across = summed_tiles(sides), summed_tiles(exchanged(across, "y"))
    opposite = lax.all_gather(opposite, "x", axis=0, tiled=True)

    by_l = jnp.stack(rolled([sides[0], sides[1], across[0], sides[2]], (4 - h) % 4))
    gram = exchanged_sum(by_l, "zl").astype(BF16)

    turned = [(q * 4 + p, p * 4 + q) for p in range(4) for q in range(4)]
    turned = lax.ppermute(gram, ("zh", "zl"), turned)
    left = lax.all_gather(gram, "zl", axis=0, tiled=True)
    right = gathered(gram, ("x", "y")).reshape(2 * pair, pair)
    left, right, above, below, turned = lax.optimization_barrier(
        (left, right, above, below, turned)
    )
    square = matmul_over_c(left, *columns(right))
    square = exchanged_sum(square.reshape(4, slab, pair), "zh")
    polynomial = (QUINTIC_B * turned.astype(F32) + QUINTIC_C * square).astype(BF16)

    polynomial = lax.all_gather(polynomial, "zl", axis=0, tiled=False)
    polynomial = jnp.concatenate(rolled([polynomial[i] for i in range(4)], h), axis=1)
    polynomial, opposite = lax.optimization_barrier((polynomial, opposite))
    polynomial = gathered(polynomial, "y").reshape(rows, 4 * pair)
    swapped = take(polynomial, "c", 1)

    blocks = (mine, above, opposite, below)
    total = add_product(False, iterate, polynomial, blocks)
    return add_product(True, total, swapped, blocks)


def solution(mesh):
    fine = Mesh(mesh.devices.reshape(tuple(SIZES.values())), tuple(SIZES))
    spec = P(("x", "zh"), ("zl", "y", "c"))
    return jax.shard_map(local, mesh=fine, in_specs=(spec,), out_specs=spec, check_vma=False)
```
